32 devices in a mesh: grp: 4 (over y, x), ctx: 8 (over z, core).
Axes of the slice: x: 2, y: 2, z: 4, core: 2. Of those that a mesh axis runs over, the one named last changes fastest.
Arguments:
- queries: bfloat16 [4096, 1792], P(('grp', 'ctx')), may hold values from -100 to 100
- keys: bfloat16 [4096, 1792], P(('grp', 'ctx')), may hold values from -5 to 5
- values: bfloat16 [4096, 1792], P(('grp', 'ctx')), may hold values from -6 to 6
- grad_out: bfloat16 [4096, 1792], P(('grp', 'ctx')), may hold values from -6 to 6
- offsets: int32 [32], replicated, may hold values from 0 to 4096, as said below
Outputs:
- grad_queries: bfloat16 [4096, 1792], P(('grp', 'ctx'))
- grad_keys: bfloat16 [4096, 1792], P(('grp', 'ctx'))
- grad_values: bfloat16 [4096, 1792], P(('grp', 'ctx'))
The draws below stay inside these ranges and needn't reach their ends.
Inputs may be any that keep to these rules, and one draw needn't show every extreme that they name: offsets[0] = 0 and the entries never fall; between consecutive entries below 4096 the difference is 128 to 384, one difference equals 384 exactly; after the last document that starts below 4096 every entry equals 4096, and that document ends at the slab's end.
All inputs are finite; a program needn't handle non-finite values.
Results may differ from the reference program's by a relative error of at most 0.0055.
Values may be sent and summed in bfloat16 or wider, within the bound.
A program may use at most 64 MiB of HBM per device.

```python
import jax
import jax.numpy as jnp
from jax import lax

HEADS = 14
HEAD_DIM = 128
TOK_DEV = 128
DOC_MAX = 384
FEATURES = 1792
MAXP = 3
TOKENS = 4096
NDOCS = 32


def key_field(key):
    base = jax.random.normal(jax.random.fold_in(key, 71), (TOKENS, HEADS * HEAD_DIM), jnp.float32)
    return jnp.clip(base, -5.0, 5.0)


def draw_keys(key, part):
    field = key_field(key)
    return field.astype(jnp.bfloat16)


def draw_queries(key, part):
    noise = jax.random.normal(jax.random.fold_in(key, 83), (TOKENS, HEADS * HEAD_DIM), jnp.float32)
    noise = jnp.clip(noise, -5.0, 5.0)
    return noise.astype(jnp.bfloat16)


def draw_offsets(key, part):
    lengths = jax.random.randint(jax.random.fold_in(key, 5), (NDOCS,), TOK_DEV, DOC_MAX + 1, dtype=jnp.int32)
    chosen = jax.random.randint(jax.random.fold_in(key, 6), (), 0, min(8, NDOCS), dtype=jnp.int32)
    lengths = jnp.where(jnp.arange(NDOCS, dtype=jnp.int32) == chosen, DOC_MAX, lengths)
    starts = jnp.cumsum(lengths) - lengths
    return jnp.minimum(starts, TOKENS).astype(jnp.int32)


def level_of(stream_key, shape, shards, low, top_value):
    def one(dim, shards_of):
        steps = jax.random.uniform(jax.random.fold_in(jax.random.fold_in(stream_key, 6), dim), (shards_of,), jnp.float32, low / len(shards), top_value / len(shards))
        return jnp.repeat(jnp.exp(steps), shape[dim] // shards_of).reshape((-1,) + (1,) * (len(shape) - dim - 1))

    level = one(*shards[0])
    for cut in shards[1:]:
        level = level * one(*cut)
    return level


def centred(rng, dims, deviation, most, shards=(), kind=jnp.bfloat16):
    gain = level_of(rng, dims, shards, -0.22, 0.18) if shards else 1.0
    entries = jax.random.normal(rng, dims, jnp.float32) * deviation * gain
    return jnp.minimum(jnp.maximum(entries, -most), most).astype(kind)


def setup_inputs(seed: int = 0) -> dict:
    streams_of = jax.random.split(jax.random.key(seed), 6)
    queries = draw_queries(jax.random.fold_in(streams_of[5], 71), 0)
    keys = draw_keys(jax.random.fold_in(streams_of[5], 71), 0)
    values = centred(streams_of[2], (TOKENS, FEATURES), 1.0, 6.0, ((0, 32),))
    grad_out = centred(streams_of[3], (TOKENS, FEATURES), 1.0, 6.0, ((0, 32),))
    offsets = draw_offsets(jax.random.fold_in(streams_of[5], 71), 0)
    return dict(queries=queries, keys=keys, values=values, grad_out=grad_out, offsets=offsets)


NEG = -1.0e30


def segments(offsets, positions, slab_len):
    found = jnp.sum((offsets[None, :] <= positions[:, None]).astype(jnp.int32), axis=1) - 1
    inside = (positions >= 0) & (positions < slab_len)
    return jnp.where(inside, found, -1)


def split_heads(block):
    return block.astype(jnp.float32).reshape(block.shape[0], HEADS, HEAD_DIM)


def rounded(block):
    return lax.optimization_barrier(block.astype(jnp.bfloat16)).astype(jnp.float32)


def pair_statistics(query_rows, grad_rows, row_segments, key_cols, value_cols, col_segments):
    allowed = (row_segments[:, None] == col_segments[None, :])[None]
    scores = jnp.einsum("qhd,khd->hqk", split_heads(query_rows), split_heads(key_cols)) * HEAD_DIM ** -0.5
    scores = jnp.where(allowed, scores, NEG)
    maximum = jnp.max(scores, axis=2)
    probs = jnp.where(allowed, jnp.exp(scores - maximum[:, :, None]), 0.0)
    dprobs = jnp.einsum("qhd,khd->hqk", split_heads(grad_rows), split_heads(value_cols))
    return maximum, jnp.sum(probs, axis=2), jnp.sum(probs * dprobs, axis=2)


def merge_statistics(first, second):
    maximum = jnp.maximum(first[0], second[0])
    scale_one = jnp.exp(first[0] - maximum)
    scale_two = jnp.exp(second[0] - maximum)
    return maximum, first[1] * scale_one + second[1] * scale_two, first[2] * scale_one + second[2] * scale_two


def finalize(statistics):
    return statistics[0] + jnp.log(statistics[1]), statistics[2] / statistics[1]


def pair_gradients(query_rows, grad_rows, row_segments, log_total, delta_rows, key_cols, value_cols, col_segments):
    allowed = (row_segments[:, None] == col_segments[None, :])[None]
    scale = HEAD_DIM ** -0.5
    scores = jnp.einsum("qhd,khd->hqk", split_heads(query_rows), split_heads(key_cols)) * scale
    probs = jnp.where(allowed, jnp.exp(scores - log_total[:, :, None]), 0.0)
    dprobs = jnp.einsum("qhd,khd->hqk", split_heads(grad_rows), split_heads(value_cols))
    dscores = jnp.where(allowed, probs * (dprobs - delta_rows[:, :, None]), 0.0)
    probs_low = rounded(probs)
    dscores_low = rounded(dscores)
    length = query_rows.shape[0]
    grad_query = jnp.einsum("hqk,khd->qhd", dscores_low, split_heads(key_cols)) * scale
    grad_key = jnp.einsum("hqk,qhd->khd", dscores_low, split_heads(query_rows)) * scale
    grad_value = jnp.einsum("hqk,qhd->khd", probs_low, split_heads(grad_rows))
    return (grad_query.reshape(length, FEATURES), grad_key.reshape(length, FEATURES), grad_value.reshape(length, FEATURES))


def reference(queries, keys, values, grad_out, offsets):
    blocks = TOKENS // TOK_DEV
    margin = MAXP * TOK_DEV
    padded_q = jnp.pad(queries, ((margin, margin), (0, 0)))
    padded_k = jnp.pad(keys, ((margin, margin), (0, 0)))
    padded_v = jnp.pad(values, ((margin, margin), (0, 0)))
    padded_o = jnp.pad(grad_out, ((margin, margin), (0, 0)))
    positions = jnp.arange(-margin, TOKENS + margin, dtype=jnp.int32)
    seg_all = segments(offsets, positions, TOKENS)

    def take(array, first):
        return lax.dynamic_slice_in_dim(array, first, TOK_DEV, 0)

    def block_statistics(block):
        base = (block + MAXP) * TOK_DEV
        query_rows = take(padded_q, base)
        grad_rows = take(padded_o, base)
        row_segments = take(seg_all, base)
        result = pair_statistics(query_rows, grad_rows, row_segments, take(padded_k, base), take(padded_v, base), row_segments)
        for distance in range(-MAXP, MAXP + 1):
            if distance != 0:
                other = base + distance * TOK_DEV
                result = merge_statistics(result, pair_statistics(query_rows, grad_rows, row_segments, take(padded_k, other), take(padded_v, other), take(seg_all, other)))
        return finalize(result)

    log_total, delta_rows = lax.map(block_statistics, jnp.arange(blocks, dtype=jnp.int32))
    padded_total = jnp.pad(log_total, ((MAXP, MAXP), (0, 0), (0, 0)))
    padded_delta = jnp.pad(delta_rows, ((MAXP, MAXP), (0, 0), (0, 0)))

    def block_gradients(block):
        base = (block + MAXP) * TOK_DEV
        query_rows = take(padded_q, base)
        grad_rows = take(padded_o, base)
        key_cols = take(padded_k, base)
        value_cols = take(padded_v, base)
        row_segments = take(seg_all, base)
        own_total = padded_total[block + MAXP]
        own_delta = padded_delta[block + MAXP]
        grad_query, grad_key, grad_value = pair_gradients(query_rows, grad_rows, row_segments, own_total, own_delta, key_cols, value_cols, row_segments)
        for distance in range(-MAXP, MAXP + 1):
            if distance != 0:
                other = base + distance * TOK_DEV
                other_block = block + MAXP + distance
                other_segments = take(seg_all, other)
                forward_terms = pair_gradients(query_rows, grad_rows, row_segments, own_total, own_delta, take(padded_k, other), take(padded_v, other), other_segments)
                grad_query = grad_query + rounded(forward_terms[0])
                reverse_terms = pair_gradients(take(padded_q, other), take(padded_o, other), other_segments, padded_total[other_block], padded_delta[other_block], key_cols, value_cols, row_segments)
                grad_key = grad_key + rounded(reverse_terms[1])
                grad_value = grad_value + rounded(reverse_terms[2])
        return (grad_query.astype(jnp.bfloat16), grad_key.astype(jnp.bfloat16), grad_value.astype(jnp.bfloat16))

    grad_queries, grad_keys, grad_values = lax.map(block_gradients, jnp.arange(blocks, dtype=jnp.int32))
    return (grad_queries.reshape(TOKENS, FEATURES), grad_keys.reshape(TOKENS, FEATURES), grad_values.reshape(TOKENS, FEATURES))
```

```python
import functools
import math

import jax
import jax.numpy as jnp
from jax import lax
from jax.experimental import pallas as pl
from jax.experimental.pallas import tpu as pltpu
from jax.sharding import PartitionSpec as P

HEAD_DIM = 128
NEG = -1e30
CHUNKS = 2
LOG2E = math.log2(math.e)
MESH = pl.DeviceIdType.MESH

K, V, Q, G = 0, 1, 2, 3
OWN, LOW, HIGH, MATE, MATE_LOW, MATE_HIGH, FAR = range(7)


def nt(a, b):
    return lax.dot_general(a, b, (((1,), (1,)), ((), ())), preferred_element_type=jnp.float32)


def nn(a, b):
    return lax.dot_general(a, b, (((1,), (0,)), ((), ())), preferred_element_type=jnp.float32)


def kernel(groups, inner, q_ref, k_ref, v_ref, g_ref, ofs_ref, gq_ref, gk_ref, gv_ref,
           buf, bias, stat, send_sem, recv_sem, loc_sem, ssend, srecv):
    rows, width = q_ref.shape
    heads = width // HEAD_DIM
    devices = groups * inner
    me = lax.axis_index("grp") * inner + lax.axis_index("ctx")
    core = lax.rem(me, 2)
    side = 2 * core - 1
    mate = me - side
    scale = HEAD_DIM ** -0.5

    def device(index):
        wrapped = lax.rem(index + devices, devices)
        return (lax.div(wrapped, inner), lax.rem(wrapped, inner))

    refs = [k_ref, v_ref, q_ref, g_ref]
    chunk_width = (heads // CHUNKS) * HEAD_DIM

    def cols(c):
        return pl.ds(c * chunk_width, chunk_width)

    def send(array, c, source, place, target):
        piece = array * CHUNKS + c
        src = refs[array].at[:, cols(c)] if source is None else buf.at[array, source, :, cols(c)]
        return pltpu.make_async_remote_copy(
            src_ref=src,
            dst_ref=buf.at[array, place, :, cols(c)],
            send_sem=send_sem.at[place, piece],
            recv_sem=recv_sem.at[place, piece],
            device_id=device(target),
            device_id_type=MESH,
        )

    def routes(array, c):
        return {
            LOW: send(array, c, None, LOW, me + 2),
            HIGH: send(array, c, None, HIGH, me - 2),
            MATE: send(array, c, None, MATE, mate),
            MATE_LOW: send(array, c, LOW, MATE_LOW, mate),
            MATE_HIGH: send(array, c, HIGH, MATE_HIGH, mate),
        }

    def start_own(array, c):
        r = routes(array, c)
        r[LOW].start()
        r[HIGH].start()
        r[MATE].start()

    def far_copy(array, c, source):
        return send(array, c, source, FAR, me + side)

    def forward(array, c):
        r = routes(array, c)
        r[LOW].wait_recv()

        @pl.when(core == 1)
        def _():
            far_copy(array, c, LOW).start()

        r[MATE_LOW].start()
        r[HIGH].wait_recv()

        @pl.when(core == 0)
        def _():
            far_copy(array, c, HIGH).start()

        r[MATE_HIGH].start()

    def wait_gathered(array, c):
        r = routes(array, c)
        r[MATE].wait_recv()
        r[MATE_LOW].wait_recv()
        r[MATE_HIGH].wait_recv()
        far_copy(array, c, LOW).wait_recv()

    def wait_sent(array, c):
        r = routes(array, c)
        for place in (LOW, HIGH, MATE, MATE_LOW, MATE_HIGH):
            r[place].wait_send()
        far_copy(array, c, LOW).wait_send()

    locals_ = [pltpu.make_async_copy(refs[a], buf.at[a, OWN], loc_sem.at[a]) for a in range(4)]
    for copy in locals_:
        copy.start()

    barrier = pltpu.get_barrier_semaphore()
    for distance in (-3, -2, -1, 1, 2, 3):
        pl.semaphore_signal(barrier, inc=1, device_id=device(me + distance), device_id_type=MESH)
    pl.semaphore_wait(barrier, 6)

    order = [(K, c) for c in range(0)]
    for c in range(CHUNKS):
        order += [(K, c), (V, c)]
    for c in range(CHUNKS):
        order += [(Q, c), (G, c)]
    for array, c in order:
        start_own(array, c)

    places = [me, me - 2, me + 2, mate, mate - 2, mate + 2, me + 3 * side]
    lane = lax.broadcasted_iota(jnp.int32, (1, rows), 1)
    across = jnp.concatenate([index * rows + lane for index in places], axis=1)
    down = me * rows + lax.broadcasted_iota(jnp.int32, (rows, 1), 0)

    def count(i, found):
        first = ofs_ref[i]
        return (found[0] + (first <= down).astype(jnp.int32),
                found[1] + (first <= across).astype(jnp.int32))

    seg_down, seg_across = lax.fori_loop(
        0, ofs_ref.shape[0], count, (jnp.full(down.shape, -1, jnp.int32), jnp.full(across.shape, -1, jnp.int32)))
    inside = (across >= 0) & (across < devices * rows)
    seg_across = jnp.where(inside, seg_across, -1)
    bias[...] = jnp.where(seg_down == seg_across, 0.0, NEG)

    for copy in locals_:
        copy.wait()

    def whole(array, col):
        return buf[array, :, :, col].reshape(7 * rows, HEAD_DIM)

    def head_col(h):
        return pl.ds(pl.multiple_of(h * HEAD_DIM, HEAD_DIM), HEAD_DIM)

    stat_lane = lax.broadcasted_iota(jnp.int32, (rows, HEAD_DIM), 1)

    def first_pass(h, totals):
        col = head_col(h)
        keys = whole(K, col)
        x = nt(buf[Q, OWN, :, col], keys) * (scale * LOG2E) + bias[...]
        top = jnp.max(x, axis=1, keepdims=True)
        e = jnp.exp2(x - top)
        norm = jnp.sum(e, axis=1, keepdims=True)
        dp = nt(buf[G, OWN, :, col], whole(V, col))
        inv = 1.0 / norm
        delta = jnp.sum(e * dp, axis=1, keepdims=True) * inv
        ds = ((e * inv) * (dp - delta)).astype(jnp.bfloat16)
        gq_ref[:, col] = (nn(ds, keys) * scale).astype(jnp.bfloat16)
        total = top + jnp.log(norm) * LOG2E
        return (jnp.where(stat_lane == h, total, totals[0]), jnp.where(stat_lane == h, delta, totals[1]))

    stat_rows = stat.shape[2]
    for c in range(CHUNKS):
        forward(K, c)
        forward(V, c)
    totals = (jnp.zeros((rows, HEAD_DIM), jnp.float32), jnp.zeros((rows, HEAD_DIM), jnp.float32))
    per = heads // CHUNKS
    for c in range(CHUNKS):
        wait_gathered(K, c)
        wait_gathered(V, c)
        totals = lax.fori_loop(c * per, (c + 1) * per, first_pass, totals)
    stat[0, 0] = totals[0].T[:stat_rows]
    stat[0, 1] = totals[1].T[:stat_rows]

    def slot(distance):
        return distance + 4 if distance < 0 else distance + 3

    stat_copies = [
        pltpu.make_async_remote_copy(
            src_ref=stat.at[0],
            dst_ref=stat.at[slot(-distance)],
            send_sem=ssend.at[slot(-distance)],
            recv_sem=srecv.at[slot(-distance)],
            device_id=device(me + distance),
            device_id_type=MESH,
        )
        for distance in (-3, -2, -1, 1, 2, 3)
    ]
    for copy in stat_copies:
        copy.start()

    for c in range(CHUNKS):
        forward(Q, c)
        forward(G, c)
    for copy in stat_copies:
        copy.wait_recv()

    by_place = [0, 2, 5, 4 - core, 3 - 2 * core, 6 - 2 * core, 1 + 5 * core]

    def second_pass(h, carry):
        col = head_col(h)
        queries, grads = whole(Q, col), whole(G, col)
        total = jnp.concatenate([stat[s, 0, pl.ds(h, 1), :] for s in by_place], axis=1)
        delta = jnp.concatenate([stat[s, 1, pl.ds(h, 1), :] for s in by_place], axis=1)
        x = nt(buf[K, OWN, :, col], queries) * (scale * LOG2E) + bias[...]
        p = jnp.exp2(x - total)
        dp = nt(buf[V, OWN, :, col], grads)
        ds = (p * (dp - delta)).astype(jnp.bfloat16)
        gv_ref[:, col] = nn(p.astype(jnp.bfloat16), grads).astype(jnp.bfloat16)
        gk_ref[:, col] = (nn(ds, queries) * scale).astype(jnp.bfloat16)
        return carry

    for c in range(CHUNKS):
        wait_gathered(Q, c)
        wait_gathered(G, c)
        lax.fori_loop(c * per, (c + 1) * per, second_pass, 0)

    for array, c in order:
        wait_sent(array, c)
    for copy in stat_copies:
        copy.wait_send()


def solution(mesh):
    groups, inner = mesh.shape["grp"], mesh.shape["ctx"]

    def on_device(queries, keys, values, grad_out, offsets):
        rows, width = queries.shape
        heads = width // HEAD_DIM
        stat_rows = -(-heads // 8) * 8
        block = jax.ShapeDtypeStruct((rows, width), jnp.bfloat16)
        pieces = 4 * CHUNKS
        return pl.pallas_call(
            functools.partial(kernel, groups, inner),
            out_shape=(block, block, block),
            in_specs=[pl.BlockSpec(memory_space=pl.ANY)] * 4 + [pl.BlockSpec(memory_space=pltpu.SMEM)],
            out_specs=[pl.BlockSpec(memory_space=pltpu.VMEM)] * 3,
            scratch_shapes=[
                pltpu.VMEM((4, 7, rows, width), jnp.bfloat16),
                pltpu.VMEM((rows, 7 * rows), jnp.float32),
                pltpu.VMEM((7, 2, stat_rows, rows), jnp.float32),
                pltpu.SemaphoreType.DMA((7, pieces)),
                pltpu.SemaphoreType.DMA((7, pieces)),
                pltpu.SemaphoreType.DMA((4,)),
                pltpu.SemaphoreType.DMA((7,)),
                pltpu.SemaphoreType.DMA((7,)),
            ],
            compiler_params=pltpu.CompilerParams(
                collective_id=0, has_side_effects=True, vmem_limit_bytes=48 * 1024 * 1024
            ),
        )(queries, keys, values, grad_out, offsets)

    split = P(("grp", "ctx"), None)
    return jax.shard_map(
        on_device,
        mesh=mesh,
        in_specs=(split, split, split, split, P()),
        out_specs=(split, split, split),
        check_vma=False,
    )
```

```python
import functools
import math

import jax
import jax.numpy as jnp
from jax import lax
from jax.experimental import pallas as pl
from jax.experimental.pallas import tpu as pltpu
from jax.sharding import PartitionSpec as P

HEAD_DIM = 128
NEG = -1e30
CHUNKS = 2
RELAYED = ((0, 0), (1, 0), (0, 1))
UPWARD_AT_FIRST = False
LOG2E = math.log2(math.e)
MESH = pl.DeviceIdType.MESH

K, V, Q, G = 0, 1, 2, 3
OWN, LOW, HIGH, MATE, MATE_LOW, MATE_HIGH, FAR = range(7)


def nt(a, b):
    return lax.dot_general(a, b, (((1,), (1,)), ((), ())), preferred_element_type=jnp.float32)


def nn(a, b):
    return lax.dot_general(a, b, (((1,), (0,)), ((), ())), preferred_element_type=jnp.float32)


def kernel(groups, inner, q_ref, k_ref, v_ref, g_ref, ofs_ref, gq_ref, gk_ref, gv_ref,
           buf, bias, stat, held, send_sem, recv_sem, loc_sem, ssend, srecv, hsend, hrecv):
    rows, width = q_ref.shape
    heads = width // HEAD_DIM
    devices = groups * inner
    me = lax.axis_index("grp") * inner + lax.axis_index("ctx")
    core = lax.rem(me, 2)
    side = 2 * core - 1
    mate = me - side
    chip, chips = lax.div(me, 2), devices // 2
    has_low, has_high = chip >= 1, chip < chips - 1
    has_far = jnp.where(core == 0, chip >= 2, chip < chips - 2)
    gives_far = has_low & has_high
    grp = lax.axis_index("grp")
    place_in_grp = lax.div(lax.axis_index("ctx"), 2)
    per_grp = inner // 2
    opens = (place_in_grp == 0) & (grp > 0)
    closes = (place_in_grp == per_grp - 1) & (grp < groups - 1)
    first, last = core, devices - 2 + core
    up_relay, down_relay = (first, last) if UPWARD_AT_FIRST else (last, first)
    scale = HEAD_DIM ** -0.5

    def device(index):
        wrapped = lax.rem(index + devices, devices)
        return (lax.div(wrapped, inner), lax.rem(wrapped, inner))

    refs = [k_ref, v_ref, q_ref, g_ref]
    chunk_width = (heads // CHUNKS) * HEAD_DIM

    def cols(c):
        return pl.ds(c * chunk_width, chunk_width)

    def send(array, c, source, place, target):
        piece = array * CHUNKS + c
        src = refs[array].at[:, cols(c)] if source is None else buf.at[array, source, :, cols(c)]
        return pltpu.make_async_remote_copy(
            src_ref=src,
            dst_ref=buf.at[array, place, :, cols(c)],
            send_sem=send_sem.at[place, piece],
            recv_sem=recv_sem.at[place, piece],
            device_id=device(target),
            device_id_type=MESH,
        )

    steps = {
        LOW: (me + 2, None, has_high, has_low),
        HIGH: (me - 2, None, has_low, has_high),
        MATE: (mate, None, None, None),
        MATE_LOW: (mate, LOW, has_low, has_low),
        MATE_HIGH: (mate, HIGH, has_high, has_high),
    }

    def where(condition, action):
        if condition is None:
            action()
        else:
            pl.when(condition)(action)

    def step(array, c, place):
        target, source, _, _ = steps[place]
        return send(array, c, source, place, target)

    def far_copy(array, c, source):
        return send(array, c, source, FAR, me + side)

    def start(array, c, place):
        where(steps[place][2], lambda: step(array, c, place).start())

    def wait_recv(array, c, place):
        where(steps[place][3], lambda: step(array, c, place).wait_recv())

    def to_relay(array, c, place):
        piece = RELAYED.index((array, c))
        boundary = grp if place == LOW else grp - 1
        return pltpu.make_async_remote_copy(
            src_ref=refs[array].at[:, cols(c)],
            dst_ref=held.at[boundary, piece],
            send_sem=send_sem.at[place, array * CHUNKS + c],
            recv_sem=hrecv.at[boundary, piece],
            device_id=device(up_relay if place == LOW else down_relay),
            device_id_type=MESH,
        )

    def from_relay(array, c, place, boundary):
        piece = RELAYED.index((array, c))
        target = (boundary + 1) * inner + core if place == LOW else boundary * inner + inner - 2 + core
        return pltpu.make_async_remote_copy(
            src_ref=held.at[boundary, piece],
            dst_ref=buf.at[array, place, :, cols(c)],
            send_sem=hsend.at[boundary, piece],
            recv_sem=recv_sem.at[place, array * CHUNKS + c],
            device_id=device(target),
            device_id_type=MESH,
        )

    def relay(array, c):
        if (array, c) not in RELAYED:
            return
        piece = RELAYED.index((array, c))
        for place, at in ((LOW, up_relay), (HIGH, down_relay)):

            @pl.when(me == at)
            def _():
                for boundary in range(groups - 1):
                    onward = from_relay(array, c, place, boundary)
                    pltpu.make_async_copy(
                        held.at[boundary, piece], held.at[boundary, piece], hrecv.at[boundary, piece]
                    ).wait()
                    onward.start()

    def relay_sent():
        for place, at in ((LOW, up_relay), (HIGH, down_relay)):

            @pl.when(me == at)
            def _():
                for array, c in RELAYED:
                    for boundary in range(groups - 1):
                        from_relay(array, c, place, boundary).wait_send()

    def start_own(array, c):
        if (array, c) in RELAYED:
            for place, crossing, present in ((LOW, closes, has_high), (HIGH, opens, has_low)):
                where(crossing, lambda: to_relay(array, c, place).start())
                where(present & jnp.logical_not(crossing), lambda: step(array, c, place).start())
        else:
            start(array, c, LOW)
            start(array, c, HIGH)
        start(array, c, MATE)

    def forward(array, c):
        relay(array, c)
        for place, onward, owner in ((LOW, MATE_LOW, 1), (HIGH, MATE_HIGH, 0)):
            wait_recv(array, c, place)
            where(gives_far & (core == owner), lambda: far_copy(array, c, place).start())
            start(array, c, onward)

    def wait_gathered(array, c):
        for place in (MATE, MATE_LOW, MATE_HIGH):
            wait_recv(array, c, place)
        where(has_far, lambda: far_copy(array, c, LOW).wait_recv())

    def wait_sent(array, c):
        for place in steps:
            where(steps[place][2], lambda: step(array, c, place).wait_send())
        where(gives_far, lambda: far_copy(array, c, LOW).wait_send())

    locals_ = [pltpu.make_async_copy(refs[a], buf.at[a, OWN], loc_sem.at[a]) for a in range(4)]
    for copy in locals_:
        copy.start()

    barrier = pltpu.get_barrier_semaphore()
    for distance in (-3, -2, -1, 1, 2, 3):
        pl.semaphore_signal(barrier, inc=1, device_id=device(me + distance), device_id_type=MESH)
    for condition, partners in (
        (opens | closes, [first, last]),
        ((me == first) | (me == last),
         [b * inner + inner - 2 + core for b in range(groups - 1)] + [(b + 1) * inner + core for b in range(groups - 1)]),
    ):

        @pl.when(condition)
        def _():
            for partner in partners:
                pl.semaphore_signal(barrier, inc=1, device_id=device(partner), device_id_type=MESH)

    expected = 6 + jnp.where(opens | closes, 2, 0) + jnp.where((me == first) | (me == last), 2 * (groups - 1), 0)
    pl.semaphore_wait(barrier, expected)

    order = []
    for c in range(CHUNKS):
        order += [(K, c), (V, c)]
    for c in range(CHUNKS):
        order += [(Q, c), (G, c)]
    for array, c in order:
        start_own(array, c)

    places = [me, me - 2, me + 2, mate, mate - 2, mate + 2, me + 3 * side]
    lane = lax.broadcasted_iota(jnp.int32, (1, rows), 1)
    across = jnp.concatenate([index * rows + lane for index in places], axis=1)
    down = me * rows + lax.broadcasted_iota(jnp.int32, (rows, 1), 0)

    def count(i, found):
        first = ofs_ref[i]
        return (found[0] + (first <= down).astype(jnp.int32),
                found[1] + (first <= across).astype(jnp.int32))

    seg_down, seg_across = lax.fori_loop(
        0, ofs_ref.shape[0], count, (jnp.full(down.shape, -1, jnp.int32), jnp.full(across.shape, -1, jnp.int32)))
    inside = (across >= 0) & (across < devices * rows)
    seg_across = jnp.where(inside, seg_across, -1)
    bias[...] = jnp.where(seg_down == seg_across, 0.0, NEG)

    def clear(place):
        def body(array, carry):
            buf[array, place] = jnp.zeros((rows, width), jnp.bfloat16)
            return carry

        lax.fori_loop(0, 4, body, 0)

    for place, present in ((LOW, has_low), (MATE_LOW, has_low), (HIGH, has_high), (MATE_HIGH, has_high), (FAR, has_far)):
        pl.when(jnp.logical_not(present))(functools.partial(clear, place))

    for copy in locals_:
        copy.wait()

    def whole(array, col):
        return buf[array, :, :, col].reshape(7 * rows, HEAD_DIM)

    def head_col(h):
        return pl.ds(pl.multiple_of(h * HEAD_DIM, HEAD_DIM), HEAD_DIM)

    stat_lane = lax.broadcasted_iota(jnp.int32, (rows, HEAD_DIM), 1)

    def first_pass(h, totals):
        col = head_col(h)
        keys = whole(K, col)
        x = nt(buf[Q, OWN, :, col], keys) * (scale * LOG2E) + bias[...]
        top = jnp.max(x, axis=1, keepdims=True)
        e = jnp.exp2(x - top)
        norm = jnp.sum(e, axis=1, keepdims=True)
        dp = nt(buf[G, OWN, :, col], whole(V, col))
        inv = 1.0 / norm
        delta = jnp.sum(e * dp, axis=1, keepdims=True) * inv
        ds = ((e * inv) * (dp - delta)).astype(jnp.bfloat16)
        gq_ref[:, col] = (nn(ds, keys) * scale).astype(jnp.bfloat16)
        total = top + jnp.log(norm) * LOG2E
        return (jnp.where(stat_lane == h, total, totals[0]), jnp.where(stat_lane == h, delta, totals[1]))

    stat_rows = stat.shape[2]
    for c in range(CHUNKS):
        forward(K, c)
        forward(V, c)
    totals = (jnp.zeros((rows, HEAD_DIM), jnp.float32), jnp.zeros((rows, HEAD_DIM), jnp.float32))
    per = heads // CHUNKS
    for c in range(CHUNKS):
        wait_gathered(K, c)
        wait_gathered(V, c)
        totals = lax.fori_loop(c * per, (c + 1) * per, first_pass, totals)
    stat[0, 0] = totals[0].T[:stat_rows]
    stat[0, 1] = totals[1].T[:stat_rows]

    def slot(distance):
        return distance + 4 if distance < 0 else distance + 3

    stat_copies = [
        pltpu.make_async_remote_copy(
            src_ref=stat.at[0],
            dst_ref=stat.at[slot(-distance)],
            send_sem=ssend.at[slot(-distance)],
            recv_sem=srecv.at[slot(-distance)],
            device_id=device(me + distance),
            device_id_type=MESH,
        )
        for distance in (-3, -2, -1, 1, 2, 3)
    ]
    for copy in stat_copies:
        copy.start()

    for c in range(CHUNKS):
        forward(Q, c)
        forward(G, c)
    for copy in stat_copies:
        copy.wait_recv()

    by_place = [0, 2, 5, 4 - core, 3 - 2 * core, 6 - 2 * core, 1 + 5 * core]

    def second_pass(h, carry):
        col = head_col(h)
        queries, grads = whole(Q, col), whole(G, col)
        total = jnp.concatenate([stat[s, 0, pl.ds(h, 1), :] for s in by_place], axis=1)
        delta = jnp.concatenate([stat[s, 1, pl.ds(h, 1), :] for s in by_place], axis=1)
        x = nt(buf[K, OWN, :, col], queries) * (scale * LOG2E) + bias[...]
        p = jnp.exp2(x - total)
        dp = nt(buf[V, OWN, :, col], grads)
        ds = (p * (dp - delta)).astype(jnp.bfloat16)
        gv_ref[:, col] = nn(p.astype(jnp.bfloat16), grads).astype(jnp.bfloat16)
        gk_ref[:, col] = (nn(ds, queries) * scale).astype(jnp.bfloat16)
        return carry

    for c in range(CHUNKS):
        wait_gathered(Q, c)
        wait_gathered(G, c)
        lax.fori_loop(c * per, (c + 1) * per, second_pass, 0)

    for array, c in order:
        wait_sent(array, c)
    relay_sent()
    for copy in stat_copies:
        copy.wait_send()


def solution(mesh):
    groups, inner = mesh.shape["grp"], mesh.shape["ctx"]

    def on_device(queries, keys, values, grad_out, offsets):
        rows, width = queries.shape
        heads = width // HEAD_DIM
        stat_rows = -(-heads // 8) * 8
        block = jax.ShapeDtypeStruct((rows, width), jnp.bfloat16)
        pieces = 4 * CHUNKS
        return pl.pallas_call(
            functools.partial(kernel, groups, inner),
            out_shape=(block, block, block),
            in_specs=[pl.BlockSpec(memory_space=pl.ANY)] * 4 + [pl.BlockSpec(memory_space=pltpu.SMEM)],
            out_specs=[pl.BlockSpec(memory_space=pltpu.VMEM)] * 3,
            scratch_shapes=[
                pltpu.VMEM((4, 7, rows, width), jnp.bfloat16),
                pltpu.VMEM((rows, 7 * rows), jnp.float32),
                pltpu.VMEM((7, 2, stat_rows, rows), jnp.float32),
                pltpu.VMEM((groups - 1, len(RELAYED), rows, (heads // CHUNKS) * HEAD_DIM), jnp.bfloat16),
                pltpu.SemaphoreType.DMA((7, pieces)),
                pltpu.SemaphoreType.DMA((7, pieces)),
                pltpu.SemaphoreType.DMA((4,)),
                pltpu.SemaphoreType.DMA((7,)),
                pltpu.SemaphoreType.DMA((7,)),
                pltpu.SemaphoreType.DMA((groups - 1, len(RELAYED))),
                pltpu.SemaphoreType.DMA((groups - 1, len(RELAYED))),
            ],
            compiler_params=pltpu.CompilerParams(
                collective_id=0, has_side_effects=True, vmem_limit_bytes=48 * 1024 * 1024
            ),
        )(queries, keys, values, grad_out, offsets)

    split = P(("grp", "ctx"), None)
    return jax.shard_map(
        on_device,
        mesh=mesh,
        in_specs=(split, split, split, split, P()),
        out_specs=(split, split, split),
        check_vma=False,
    )
```

```python
import functools
import math

import jax
import jax.numpy as jnp
from jax import lax
from jax.experimental import pallas as pl
from jax.experimental.pallas import tpu as pltpu
from jax.sharding import PartitionSpec as P

HEAD_DIM = 128
NEG = -1e30
CHUNKS = 2
RELAYED = ((0, 0), (1, 0), (0, 1))
UPWARD_AT_FIRST = False
LOG2E = math.log2(math.e)
MESH = pl.DeviceIdType.MESH

K, V, Q, G = 0, 1, 2, 3
OWN, LOW, HIGH, MATE, MATE_LOW, MATE_HIGH, FAR = range(7)


def nt(a, b):
    return lax.dot_general(a, b, (((1,), (1,)), ((), ())), preferred_element_type=jnp.float32)


def nn(a, b):
    return lax.dot_general(a, b, (((1,), (0,)), ((), ())), preferred_element_type=jnp.float32)


def kernel(groups, inner, q_ref, k_ref, v_ref, g_ref, ofs_ref, gq_ref, gk_ref, gv_ref,
           buf, bias, stat, held, send_sem, recv_sem, loc_sem, ssend, srecv, hsend, hrecv):
    rows, width = q_ref.shape
    heads = width // HEAD_DIM
    devices = groups * inner
    me = lax.axis_index("grp") * inner + lax.axis_index("ctx")
    core = lax.rem(me, 2)
    side = 2 * core - 1
    mate = me - side
    chip, chips = lax.div(me, 2), devices // 2
    has_low, has_high = chip >= 1, chip < chips - 1
    has_far = jnp.where(core == 0, chip >= 2, chip < chips - 2)
    gives_far = has_low & has_high
    grp = lax.axis_index("grp")
    place_in_grp = lax.div(lax.axis_index("ctx"), 2)
    per_grp = inner // 2
    opens = (place_in_grp == 0) & (grp > 0)
    closes = (place_in_grp == per_grp - 1) & (grp < groups - 1)
    first, last = core, devices - 2 + core
    up_relay, down_relay = (first, last) if UPWARD_AT_FIRST else (last, first)
    scale = HEAD_DIM ** -0.5

    def device(index):
        wrapped = lax.rem(index + devices, devices)
        return (lax.div(wrapped, inner), lax.rem(wrapped, inner))

    refs = [k_ref, v_ref, q_ref, g_ref]
    chunk_width = (heads // CHUNKS) * HEAD_DIM

    def cols(c):
        return pl.ds(c * chunk_width, chunk_width)

    def send(array, c, source, place, target):
        piece = array * CHUNKS + c
        src = refs[array].at[:, cols(c)] if source is None else buf.at[array, source, :, cols(c)]
        return pltpu.make_async_remote_copy(
            src_ref=src,
            dst_ref=buf.at[array, place, :, cols(c)],
            send_sem=send_sem.at[place, piece],
            recv_sem=recv_sem.at[place, piece],
            device_id=device(target),
            device_id_type=MESH,
        )

    steps = {
        LOW: (me + 2, None, has_high, has_low),
        HIGH: (me - 2, None, has_low, has_high),
        MATE: (mate, None, None, None),
        MATE_LOW: (mate, LOW, has_low, has_low),
        MATE_HIGH: (mate, HIGH, has_high, has_high),
    }

    def where(condition, action):
        if condition is None:
            action()
        else:
            pl.when(condition)(action)

    def step(array, c, place):
        target, source, _, _ = steps[place]
        return send(array, c, source, place, target)

    def far_copy(array, c, source):
        return send(array, c, source, FAR, me + side)

    def start(array, c, place):
        where(steps[place][2], lambda: step(array, c, place).start())

    def wait_recv(array, c, place):
        where(steps[place][3], lambda: step(array, c, place).wait_recv())

    def to_relay(array, c, place):
        piece = RELAYED.index((array, c))
        boundary = grp if place == LOW else grp - 1
        return pltpu.make_async_remote_copy(
            src_ref=refs[array].at[:, cols(c)],
            dst_ref=held.at[boundary, piece],
            send_sem=send_sem.at[place, array * CHUNKS + c],
            recv_sem=hrecv.at[boundary, piece],
            device_id=device(up_relay if place == LOW else down_relay),
            device_id_type=MESH,
        )

    def from_relay(array, c, place, boundary):
        piece = RELAYED.index((array, c))
        target = (boundary + 1) * inner + core if place == LOW else boundary * inner + inner - 2 + core
        return pltpu.make_async_remote_copy(
            src_ref=held.at[boundary, piece],
            dst_ref=buf.at[array, place, :, cols(c)],
            send_sem=hsend.at[boundary, piece],
            recv_sem=recv_sem.at[place, array * CHUNKS + c],
            device_id=device(target),
            device_id_type=MESH,
        )

    def relay(array, c):
        if (array, c) not in RELAYED:
            return
        piece = RELAYED.index((array, c))
        for place, at in ((LOW, up_relay), (HIGH, down_relay)):

            @pl.when(me == at)
            def _():
                for boundary in range(groups - 1):
                    onward = from_relay(array, c, place, boundary)
                    pltpu.make_async_copy(
                        held.at[boundary, piece], held.at[boundary, piece], hrecv.at[boundary, piece]
                    ).wait()
                    onward.start()

    def relay_sent():
        for place, at in ((LOW, up_relay), (HIGH, down_relay)):

            @pl.when(me == at)
            def _():
                for array, c in RELAYED:
                    for boundary in range(groups - 1):
                        from_relay(array, c, place, boundary).wait_send()

    def start_own(array, c):
        if (array, c) in RELAYED:
            for place, crossing, present in ((LOW, closes, has_high), (HIGH, opens, has_low)):
                where(crossing, lambda: to_relay(array, c, place).start())
                where(present & jnp.logical_not(crossing), lambda: step(array, c, place).start())
        else:
            start(array, c, LOW)
            start(array, c, HIGH)
        start(array, c, MATE)

    def forward(array, c):
        relay(array, c)
        for place, onward, owner in ((LOW, MATE_LOW, 1), (HIGH, MATE_HIGH, 0)):
            wait_recv(array, c, place)
            where(gives_far & (core == owner), lambda: far_copy(array, c, place).start())
            start(array, c, onward)

    def wait_gathered(array, c):
        for place in (MATE, MATE_LOW, MATE_HIGH):
            wait_recv(array, c, place)
        where(has_far, lambda: far_copy(array, c, LOW).wait_recv())

    def wait_sent(array, c):
        for place in steps:
            where(steps[place][2], lambda: step(array, c, place).wait_send())
        where(gives_far, lambda: far_copy(array, c, LOW).wait_send())

    locals_ = [pltpu.make_async_copy(refs[a], buf.at[a, OWN], loc_sem.at[a]) for a in range(4)]
    for copy in locals_:
        copy.start()

    barrier = pltpu.get_barrier_semaphore()
    for distance in (-3, -2, -1, 1, 2, 3):
        pl.semaphore_signal(barrier, inc=1, device_id=device(me + distance), device_id_type=MESH)
    for condition, partners in (
        (opens | closes, [first, last]),
        ((me == first) | (me == last),
         [b * inner + inner - 2 + core for b in range(groups - 1)] + [(b + 1) * inner + core for b in range(groups - 1)]),
    ):

        @pl.when(condition)
        def _():
            for partner in partners:
                pl.semaphore_signal(barrier, inc=1, device_id=device(partner), device_id_type=MESH)

    expected = 6 + jnp.where(opens | closes, 2, 0) + jnp.where((me == first) | (me == last), 2 * (groups - 1), 0)
    pl.semaphore_wait(barrier, expected)

    order = []
    for c in range(CHUNKS):
        order += [(K, c), (V, c)]
    for c in range(CHUNKS):
        order += [(Q, c), (G, c)]
    for array, c in order:
        start_own(array, c)

    places = [me, me - 2, me + 2, mate, mate - 2, mate + 2, me + 3 * side]
    lane = lax.broadcasted_iota(jnp.int32, (1, rows), 1)
    across = jnp.concatenate([index * rows + lane for index in places], axis=1)
    down = me * rows + lax.broadcasted_iota(jnp.int32, (rows, 1), 0)

    def count(i, found):
        first = ofs_ref[i]
        return (found[0] + (first <= down).astype(jnp.int32),
                found[1] + (first <= across).astype(jnp.int32))

    seg_down, seg_across = lax.fori_loop(
        0, ofs_ref.shape[0], count, (jnp.full(down.shape, -1, jnp.int32), jnp.full(across.shape, -1, jnp.int32)))
    inside = (across >= 0) & (across < devices * rows)
    seg_across = jnp.where(inside, seg_across, -1)
    bias[...] = jnp.where(seg_down == seg_across, 0.0, NEG)

    def clear(place):
        def body(array, carry):
            buf[array, place] = jnp.zeros((rows, width), jnp.bfloat16)
            return carry

        lax.fori_loop(0, 4, body, 0)

    for place, present in ((LOW, has_low), (MATE_LOW, has_low), (HIGH, has_high), (MATE_HIGH, has_high), (FAR, has_far)):
        pl.when(jnp.logical_not(present))(functools.partial(clear, place))

    for copy in locals_:
        copy.wait()

    def whole(array, col):
        return buf[array, :, :, col].reshape(7 * rows, HEAD_DIM)

    def head_col(h):
        return pl.ds(pl.multiple_of(h * HEAD_DIM, HEAD_DIM), HEAD_DIM)

    stat_lane = lax.broadcasted_iota(jnp.int32, (rows, HEAD_DIM), 1)

    def first_pass(h, totals):
        col = head_col(h)
        keys = whole(K, col)
        x = nt(buf[Q, OWN, :, col], keys) * (scale * LOG2E) + bias[...]
        top = jnp.max(x, axis=1, keepdims=True)
        e = jnp.exp2(x - top)
        norm = jnp.sum(e, axis=1, keepdims=True)
        dp = nt(buf[G, OWN, :, col], whole(V, col))
        inv = 1.0 / norm
        delta = jnp.sum(e * dp, axis=1, keepdims=True) * inv
        ds = ((e * inv) * (dp - delta)).astype(jnp.bfloat16)
        gq_ref[:, col] = (nn(ds, keys) * scale).astype(jnp.bfloat16)
        total = top + jnp.log(norm) * LOG2E
        return (jnp.where(stat_lane == h, total, totals[0]), jnp.where(stat_lane == h, delta, totals[1]))

    stat_rows = stat.shape[2]
    for c in range(CHUNKS):
        forward(K, c)
        forward(V, c)
    totals = (jnp.zeros((rows, HEAD_DIM), jnp.float32), jnp.zeros((rows, HEAD_DIM), jnp.float32))
    per = heads // CHUNKS
    for c in range(CHUNKS):
        wait_gathered(K, c)
        wait_gathered(V, c)
        totals = lax.fori_loop(c * per, (c + 1) * per, first_pass, totals)
        if c < CHUNKS - 1:
            forward(Q, c)
            forward(G, c)
    stat[0, 0] = totals[0].T[:stat_rows]
    stat[0, 1] = totals[1].T[:stat_rows]

    def slot(distance):
        return distance + 4 if distance < 0 else distance + 3

    stat_copies = [
        pltpu.make_async_remote_copy(
            src_ref=stat.at[0],
            dst_ref=stat.at[slot(-distance)],
            send_sem=ssend.at[slot(-distance)],
            recv_sem=srecv.at[slot(-distance)],
            device_id=device(me + distance),
            device_id_type=MESH,
        )
        for distance in (-3, -2, -1, 1, 2, 3)
    ]
    for copy in stat_copies:
        copy.start()

    forward(Q, CHUNKS - 1)
    forward(G, CHUNKS - 1)
    for copy in stat_copies:
        copy.wait_recv()

    by_place = [0, 2, 5, 4 - core, 3 - 2 * core, 6 - 2 * core, 1 + 5 * core]

    def second_pass(h, carry):
        col = head_col(h)
        queries, grads = whole(Q, col), whole(G, col)
        total = jnp.concatenate([stat[s, 0, pl.ds(h, 1), :] for s in by_place], axis=1)
        delta = jnp.concatenate([stat[s, 1, pl.ds(h, 1), :] for s in by_place], axis=1)
        x = nt(buf[K, OWN, :, col], queries) * (scale * LOG2E) + bias[...]
        p = jnp.exp2(x - total)
        dp = nt(buf[V, OWN, :, col], grads)
        ds = (p * (dp - delta)).astype(jnp.bfloat16)
        gv_ref[:, col] = nn(p.astype(jnp.bfloat16), grads).astype(jnp.bfloat16)
        gk_ref[:, col] = (nn(ds, queries) * scale).astype(jnp.bfloat16)
        return carry

    for c in range(CHUNKS):
        wait_gathered(Q, c)
        wait_gathered(G, c)
        lax.fori_loop(c * per, (c + 1) * per, second_pass, 0)

    for array, c in order:
        wait_sent(array, c)
    relay_sent()
    for copy in stat_copies:
        copy.wait_send()


def solution(mesh):
    groups, inner = mesh.shape["grp"], mesh.shape["ctx"]

    def on_device(queries, keys, values, grad_out, offsets):
        rows, width = queries.shape
        heads = width // HEAD_DIM
        stat_rows = -(-heads // 8) * 8
        block = jax.ShapeDtypeStruct((rows, width), jnp.bfloat16)
        pieces = 4 * CHUNKS
        return pl.pallas_call(
            functools.partial(kernel, groups, inner),
            out_shape=(block, block, block),
            in_specs=[pl.BlockSpec(memory_space=pl.ANY)] * 4 + [pl.BlockSpec(memory_space=pltpu.SMEM)],
            out_specs=[pl.BlockSpec(memory_space=pltpu.VMEM)] * 3,
            scratch_shapes=[
                pltpu.VMEM((4, 7, rows, width), jnp.bfloat16),
                pltpu.VMEM((rows, 7 * rows), jnp.float32),
                pltpu.VMEM((7, 2, stat_rows, rows), jnp.float32),
                pltpu.VMEM((groups - 1, len(RELAYED), rows, (heads // CHUNKS) * HEAD_DIM), jnp.bfloat16),
                pltpu.SemaphoreType.DMA((7, pieces)),
                pltpu.SemaphoreType.DMA((7, pieces)),
                pltpu.SemaphoreType.DMA((4,)),
                pltpu.SemaphoreType.DMA((7,)),
                pltpu.SemaphoreType.DMA((7,)),
                pltpu.SemaphoreType.DMA((groups - 1, len(RELAYED))),
                pltpu.SemaphoreType.DMA((groups - 1, len(RELAYED))),
            ],
            compiler_params=pltpu.CompilerParams(
                collective_id=0, has_side_effects=True, vmem_limit_bytes=48 * 1024 * 1024
            ),
        )(queries, keys, values, grad_out, offsets)

    split = P(("grp", "ctx"), None)
    return jax.shard_map(
        on_device,
        mesh=mesh,
        in_specs=(split, split, split, split, P()),
        out_specs=(split, split, split),
        check_vma=False,
    )
```
